32 devices in a mesh: section: 8 (over z, y), dp: 4 (over x, core).
Axes of the slice: x: 2, y: 2, z: 4, core: 2. Of those that a mesh axis runs over, the one named last changes fastest.
Arguments:
- w_first: bfloat16 [8, 512, 2048], P('section'), may hold values from -0.25 to 0.25
- w_second_t: bfloat16 [8, 512, 2048], P('section'), may hold values from -0.125 to 0.125
- m_first: float32 [8, 512, 2048], P('section', 'dp'), may hold values from -6 to 6
- v_first: float32 [8, 512, 2048], P('section', 'dp'), may hold values from 10 to 100
- m_second: float32 [8, 512, 2048], P('section', 'dp'), may hold values from -6 to 6
- v_second: float32 [8, 512, 2048], P('section', 'dp'), may hold values from 10 to 100
- lengths: int32 [4, 10], replicated, may hold values from 1 to 256, 1280 in all within a row
- act_arrive: bfloat16 [4, 8, 256, 512], P('dp', 'section'), may hold values from -6 to 6
- cot_arrive: bfloat16 [4, 8, 256, 512], P('dp', 'section'), may hold values from -6 to 6
- embed_next: bfloat16 [4, 2, 256, 512], P('dp'), may hold values from -6 to 6
- loss_cot: bfloat16 [4, 2, 256, 512], P('dp'), may hold values from -6 to 6
- stash: bfloat16 [4, 8, 3, 256, 512], P('dp', 'section'), may hold values from -6 to 6
Outputs:
- act_leave: bfloat16 [4, 8, 3, 256, 512], P('dp', 'section')
- cot_leave: bfloat16 [4, 8, 3, 256, 512], P('dp', 'section')
- step_first: float32 [8, 512, 2048], P('section', 'dp')
- step_second: float32 [8, 512, 2048], P('section', 'dp')
The draws below stay inside these ranges and needn't reach their ends.
Inputs may be any that keep to these rules, and one draw needn't show every extreme that they name: lengths[g, m] counts the live rows of microbatch m of data group g; each row of lengths sums to 1280 and its largest entry is 256.
All inputs are finite; a program needn't handle non-finite values.
Results may differ from the reference program's by a relative error of at most 0.007.
Values may be sent and summed in bfloat16 or wider, within the bound.
A program may use at most 128 MiB of HBM per device.

```python
import math
import jax
import jax.numpy as jnp
import numpy as np
from jax import lax

D = 512
FF = 2048
CAP = 256
TICKS = 3
SECTIONS = 8
GROUPS = 4
MB = 10
LEN_MEAN = 128


def shard_levels(key, shape, pieces, smallest, high):
    factor_of = 1.0
    for dim, shards_of in pieces:
        heights = jax.random.uniform(jax.random.fold_in(jax.random.fold_in(key, 6), dim), (shards_of,), jnp.float32, smallest / len(pieces), high / len(pieces))
        factor_of = factor_of * jnp.repeat(jnp.exp(heights), shape[dim] // shards_of).reshape((-1,) + (1,) * (len(shape) - 1 - dim))
    return factor_of


def split_up(count, total, most, slope):
    portions = [(1 << 20) // math.isqrt(standing ** slope) + 1 for standing in range(2, count + 1)]
    rest, counts = total - most - (count - 1), [1] * (count - 1)
    while rest > 0:
        candidates = [i for i in range(count - 1) if counts[i] < most]
        whole, budget = sum([portions[i] for i in candidates]), rest
        for i in candidates:
            addition = min(most - counts[i], max(1, budget * portions[i] // whole), rest)
            counts[i] = counts[i] + addition
            rest = rest - addition
    return np.array([most] + counts)


def ragged(stream_key, amount, total, most, slope):
    if amount == 2:
        one = jax.random.randint(stream_key, (), max(1, total - most), min(most, total - 1) + 1)
        return jnp.stack([one, total - one])
    tallies = jnp.asarray(split_up(amount, total, most, slope), jnp.int32)
    pairs = (amount - 1) // 2
    source_of, taker = tallies[1:1 + 2 * pairs:2], tallies[2:2 + 2 * pairs:2]
    slack = jnp.minimum(source_of - 1, most - taker)
    passed = jax.random.randint(jax.random.fold_in(stream_key, 1), (pairs,), 0, 1 << 20) % (slack + 1)
    tallies = tallies.at[1:1 + 2 * pairs:2].set(source_of - passed).at[2:2 + 2 * pairs:2].set(taker + passed)
    return tallies[jax.random.permutation(jax.random.fold_in(stream_key, 2), amount)]


def bell_draw(rng, shape, spread, bound, shards=(), kind=jnp.bfloat16):
    result = spread * jax.random.normal(rng, shape, jnp.float32)
    if shards:
        result = result * shard_levels(rng, shape, shards, -0.22, 0.18)
    return jnp.clip(result, -bound, bound).astype(kind)


def setup_inputs(seed: int = 0) -> dict:
    keys = jax.random.split(jax.random.key(seed), 13)
    w_first = bell_draw(keys[0], (SECTIONS, D, FF), D ** -0.5, 0.25, ((0, 8),))
    w_second_t = bell_draw(keys[1], (SECTIONS, D, FF), FF ** -0.5, 0.125, ((0, 8),))
    m_first = bell_draw(keys[2], (SECTIONS, D, FF), 1.0, 6.0, ((0, 8), (1, 4)), jnp.float32)
    v_first = jnp.clip(jnp.exp(math.log(100.0) - 2.3025851 * jax.random.uniform(keys[3], (SECTIONS, D, FF), jnp.float32) ** shard_levels(keys[3], (SECTIONS, D, FF), ((0, 8), (1, 4)), -0.2, 0.2)), 10.0, 100.0)
    m_second = bell_draw(keys[4], (SECTIONS, D, FF), 1.0, 6.0, ((0, 8), (1, 4)), jnp.float32)
    v_second = jnp.clip(jnp.exp(math.log(100.0) - 2.3025851 * jax.random.uniform(keys[5], (SECTIONS, D, FF), jnp.float32) ** shard_levels(keys[5], (SECTIONS, D, FF), ((0, 8), (1, 4)), -0.2, 0.2)), 10.0, 100.0)
    lengths = jax.vmap(lambda own: ragged(own, MB, LEN_MEAN * MB, CAP, 2))(jax.random.split(keys[6], GROUPS)).reshape((GROUPS, MB)).astype(jnp.int32)
    act_arrive = bell_draw(keys[7], (GROUPS, SECTIONS, CAP, D), 1.0, 6.0, ((0, 4), (1, 8)))
    cot_arrive = bell_draw(keys[8], (GROUPS, SECTIONS, CAP, D), 1.0, 6.0, ((0, 4), (1, 8)))
    embed_next = bell_draw(keys[9], (GROUPS, TICKS - 1, CAP, D), 1.0, 6.0, ((0, 4),))
    loss_cot = bell_draw(keys[10], (GROUPS, TICKS - 1, CAP, D), 1.0, 6.0, ((0, 4),))
    stash = bell_draw(keys[11], (GROUPS, SECTIONS, TICKS, CAP, D), 1.0, 6.0, ((0, 4), (1, 8)))
    return {"w_first": w_first, "w_second_t": w_second_t, "m_first": m_first, "v_first": v_first, "m_second": m_second, "v_second": v_second, "lengths": lengths, "act_arrive": act_arrive, "cot_arrive": cot_arrive, "embed_next": embed_next, "loss_cot": loss_cot, "stash": stash}


NORM_EPS = 1e-05
ADAM_EPS = 1e-08
beta_one = 0.9
beta_two = 0.98
correct_one = 1.0 - 0.9 ** 10
correct_two = 1.0 - 0.98 ** 10
gelu_coeff = 0.7978845608
cubic_coeff = 0.044715
residual_alpha = 1500.0 ** 0.25
contract_rows = (((0,), (0,)), ((), ()))
contract_cols = (((1,), (1,)), ((), ()))

def gelu_parts(pre_act):
    inner_arg = gelu_coeff * (pre_act + cubic_coeff * pre_act * pre_act * pre_act)
    tangent = jnp.tanh(inner_arg)
    gelu_value = 0.5 * pre_act * (1.0 + tangent)
    gelu_slope = 0.5 * (1.0 + tangent) + 0.5 * pre_act * (1.0 - tangent * tangent) * gelu_coeff * (1.0 + 3.0 * cubic_coeff * pre_act * pre_act)
    return (gelu_value, gelu_slope)

def layer_forward(inputs, weight_first, weight_second, residual_scale):
    pre_act = jnp.dot(inputs, weight_first, preferred_element_type=jnp.float32)
    gelu_value, gelu_slope = gelu_parts(pre_act)
    hidden = gelu_value.astype(jnp.bfloat16)
    branch = lax.dot_general(hidden, weight_second, contract_cols, preferred_element_type=jnp.float32)
    summed = residual_scale * inputs.astype(jnp.float32) + branch
    center = summed - lax.optimization_barrier(jnp.mean(summed, axis=1, keepdims=True))
    inv_std = lax.rsqrt(lax.optimization_barrier(jnp.mean(center * center, axis=1, keepdims=True)) + NORM_EPS)
    return (gelu_slope, hidden, center * inv_std, inv_std)

def live_mask(inputs, length, first_row):
    return lax.broadcasted_iota(jnp.int32, (inputs.shape[0], 1), 0) + first_row < length

def section_forward(inputs, weight_first, weight_second, length, first_row, residual_scale):
    normed = layer_forward(inputs, weight_first, weight_second, residual_scale)[2]
    return jnp.where(live_mask(inputs, length, first_row), normed, 0.0).astype(jnp.bfloat16)

def section_backward(inputs, cotangent, weight_first, weight_second, length, first_row, residual_scale):
    gelu_slope, hidden, normed, inv_std = layer_forward(inputs, weight_first, weight_second, residual_scale)
    grad_out = jnp.where(live_mask(inputs, length, first_row), cotangent.astype(jnp.float32), 0.0)
    grad_sum = inv_std * (grad_out - lax.optimization_barrier(jnp.mean(grad_out, axis=1, keepdims=True)) - normed * lax.optimization_barrier(jnp.mean(grad_out * normed, axis=1, keepdims=True)))
    grad_sum_b = grad_sum.astype(jnp.bfloat16)
    grad_hidden = jnp.dot(grad_sum_b, weight_second, preferred_element_type=jnp.float32)
    grad_pre = (grad_hidden * gelu_slope).astype(jnp.bfloat16)
    grad_in = (residual_scale * grad_sum + lax.dot_general(grad_pre, weight_first, contract_cols, preferred_element_type=jnp.float32)).astype(jnp.bfloat16)
    return (grad_in, grad_pre, grad_sum_b, hidden)

def adam_step(gradient, moment, second):
    moment_new = beta_one * moment + (1.0 - beta_one) * gradient
    second_new = beta_two * second + (1.0 - beta_two) * gradient * gradient
    return moment_new / correct_one / (jnp.sqrt(second_new / correct_two) + ADAM_EPS)

def reference(w_first, w_second_t, m_first, v_first, m_second, v_second, lengths, act_arrive, cot_arrive, embed_next, loss_cot, stash):
    residual_scale = residual_alpha
    sections = jnp.arange(SECTIONS, dtype=jnp.int32)

    def forward_item(section_item):
        return section_forward(section_item[0], section_item[1], section_item[2], section_item[3], 0, residual_scale)

    def backward_item(section_item):
        saved_in, cot_in, weight_first, weight_second, length = section_item
        grad_in, grad_pre, grad_sum_b, hidden = section_backward(saved_in, cot_in, weight_first, weight_second, length, 0, residual_scale)
        term_first = lax.dot_general(saved_in, grad_pre, contract_rows, preferred_element_type=jnp.float32)
        term_second = lax.dot_general(grad_sum_b, hidden, contract_rows, preferred_element_type=jnp.float32)
        return (grad_in, term_first, term_second)

    def one_group(sums_carry, group_data):
        group_lengths, arrive_rows, embeds, cot_rows, losses, saved_inputs = group_data
        inputs = arrive_rows
        forward_outs = []
        for tick_index in range(TICKS):
            tick_lengths = group_lengths[tick_index - sections + SECTIONS - 1]
            outputs = lax.map(forward_item, (inputs, w_first, w_second_t, tick_lengths))
            forward_outs.append(outputs)
            if tick_index + 1 < TICKS:
                inputs = jnp.concatenate([embeds[tick_index][None], outputs[:-1]], axis=0)
        cotangent = cot_rows
        backward_outs = []
        part_first = jnp.zeros((SECTIONS, D, FF), jnp.float32)
        part_second = jnp.zeros((SECTIONS, D, FF), jnp.float32)
        for tick_index in range(TICKS):
            tick_lengths = group_lengths[tick_index + sections]
            grads_in, term_first, term_second = lax.map(backward_item, (saved_inputs[:, tick_index], cotangent, w_first, w_second_t, tick_lengths))
            part_first = part_first + term_first
            part_second = part_second + term_second
            backward_outs.append(grads_in)
            if tick_index + 1 < TICKS:
                cotangent = jnp.concatenate([grads_in[1:], losses[tick_index][None]], axis=0)
        rounded_first = lax.optimization_barrier(part_first.astype(jnp.bfloat16)).astype(jnp.float32)
        rounded_second = lax.optimization_barrier(part_second.astype(jnp.bfloat16)).astype(jnp.float32)
        new_carry = (sums_carry[0] + rounded_first, sums_carry[1] + rounded_second)
        return (new_carry, (jnp.stack(forward_outs, axis=1), jnp.stack(backward_outs, axis=1)))
    start_carry = (jnp.zeros((SECTIONS, D, FF), jnp.float32), jnp.zeros((SECTIONS, D, FF), jnp.float32))
    sums_final, leaving = lax.scan(one_group, start_carry, (lengths, act_arrive, embed_next, cot_arrive, loss_cot, stash))
    step_first = adam_step(sums_final[0], m_first, v_first)
    step_second = adam_step(sums_final[1], m_second, v_second)
    return (leaving[0], leaving[1], step_first, step_second)
```

```python
import functools

import jax
import jax.numpy as jnp
from jax import lax
from jax.experimental import pallas as pl
from jax.experimental.pallas import tpu as pltpu
from jax.sharding import PartitionSpec as P

NORM_EPS = 1e-05
ADAM_EPS = 1e-08
beta_one = 0.9
beta_two = 0.98
correct_one = 1.0 - 0.9**10
correct_two = 1.0 - 0.98**10
gelu_coeff = 0.7978845608
cubic_coeff = 0.044715
residual_alpha = 1500.0**0.25
NT = (((1,), (1,)), ((), ()))
BF = jnp.bfloat16
F32 = jnp.float32
MESH = pl.DeviceIdType.MESH


def gelu(pre, slope):
    square = pre * pre
    tangent = jnp.tanh(pre * (gelu_coeff + (gelu_coeff * cubic_coeff) * square))
    half = 0.5 * pre
    cdf = 1.0 + tangent
    hidden = (half * cdf).astype(BF)
    if not slope:
        return hidden, None
    bent = gelu_coeff + (3.0 * gelu_coeff * cubic_coeff) * square
    return hidden, 0.5 * cdf + (half * bent) * (1.0 - tangent * tangent)


def dot(a, b):
    return jnp.dot(a, b, preferred_element_type=F32)


def dot_nt(a, b):
    return lax.dot_general(a, b, NT, preferred_element_type=F32)


def kernel(
    sections, groups, ticks, chunk,
    w1_h, w2_h, m1_h, v1_h, m2_h, v2_h, lengths, act_h, cot_h, embed_h, loss_h, stash_h,
    act_o, cot_o, s1_o, s2_o,
    w1, w2, moments, x_in, a_in, c_in, r_x, r_g, act_b, cot_b, g_b, slopes, normed, inv_std,
    f_hid, hid, gp, xt, gt, acc, out_x, in_x, steps,
    w_sem, mom_sem, x_sem, a_sem, c_sem, o_sem, st_sem,
    hop_s, hop_r, rx_s, rx_r, rg_s, rg_r, ex_s, ex_r,
):
    s = lax.axis_index("section")
    me = lax.axis_index("dp")
    chips = groups // 2
    chip, core = me // 2, me % 2
    sibling = me + 1 - 2 * core
    width, units = w1.shape
    cap = x_in.shape[1]
    rows = width // chips
    own = rows // 2
    chunks = units // chunk
    first, last = s == 0, s == sections - 1
    nxt = jnp.minimum(s + 1, sections - 1)
    prv = jnp.maximum(s - 1, 0)
    partners = [lax.rem(chip + p, chips) * 2 + core for p in range(1, chips)]

    barrier = pltpu.get_barrier_semaphore()

    @pl.when(jnp.logical_not(first))
    def _():
        pl.semaphore_signal(barrier, inc=1, device_id={"section": prv}, device_id_type=MESH)

    @pl.when(jnp.logical_not(last))
    def _():
        pl.semaphore_signal(barrier, inc=1, device_id={"section": nxt}, device_id_type=MESH)

    for other in partners + [sibling]:
        pl.semaphore_signal(barrier, inc=1, device_id={"dp": other}, device_id_type=MESH)

    loads_x = [pltpu.make_async_copy(stash_h.at[0, 0, k], x_in.at[k], x_sem.at[k]) for k in range(ticks)]
    load_w1 = pltpu.make_async_copy(w1_h.at[0], w1, w_sem.at[0])
    load_w2 = pltpu.make_async_copy(w2_h.at[0], w2, w_sem.at[1])
    loads_a = [pltpu.make_async_copy(act_h.at[0, 0], a_in.at[0], a_sem.at[0])]
    loads_c = [pltpu.make_async_copy(cot_h.at[0, 0], c_in.at[0], c_sem.at[0])]
    for k in range(1, ticks):
        loads_a.append(pltpu.make_async_copy(embed_h.at[0, k - 1], a_in.at[k], a_sem.at[k]))
        loads_c.append(pltpu.make_async_copy(loss_h.at[0, k - 1], c_in.at[k], c_sem.at[k]))
    loads_m = [
        pltpu.make_async_copy(h.at[0], moments.at[i], mom_sem.at[i])
        for i, h in enumerate((m1_h, v1_h, m2_h, v2_h))
    ]
    loads_x[0].start()
    load_w1.start()
    load_w2.start()
    loads_c[0].start()
    loads_a[0].start()
    for k in range(1, ticks):
        loads_x[k].start()

    @pl.when(first)
    def _():
        for k in range(1, ticks):
            loads_a[k].start()

    @pl.when(last)
    def _():
        for k in range(1, ticks):
            loads_c[k].start()

    for load in loads_m:
        load.start()

    pl.semaphore_wait(
        barrier, chips + jnp.where(first, 0, 1) + jnp.where(last, 0, 1)
    )

    def send_tick(k, src, dst, send, recv):
        return [
            pltpu.make_async_remote_copy(
                src_ref=src, dst_ref=dst.at[k, p], send_sem=send.at[k, p], recv_sem=recv.at[k, p],
                device_id={"dp": other}, device_id_type=MESH,
            )
            for p, other in enumerate(partners)
        ]

    sends_x = [send_tick(k, stash_h.at[0, 0, k], r_x, rx_s, rx_r) for k in range(ticks)]
    sends_g = [send_tick(k, g_b.at[k], r_g, rg_s, rg_r) for k in range(ticks)]
    for copies in sends_x:
        for copy in copies:
            copy.start()

    def hop(src, dst, i, to):
        return pltpu.make_async_remote_copy(
            src_ref=src, dst_ref=dst, send_sem=hop_s.at[i], recv_sem=hop_r.at[i],
            device_id={"section": to}, device_id_type=MESH,
        )

    hops_a = [hop(act_b.at[k], a_in.at[k + 1], k, nxt) for k in range(ticks - 1)]
    hops_c = [hop(cot_b.at[k], c_in.at[k + 1], ticks - 1 + k, prv) for k in range(ticks - 1)]
    outs_a = [pltpu.make_async_copy(act_b.at[k], act_o.at[k], o_sem.at[k]) for k in range(ticks)]
    outs_c = [pltpu.make_async_copy(cot_b.at[k], cot_o.at[k], o_sem.at[ticks + k]) for k in range(ticks)]

    row_ids = lax.broadcasted_iota(jnp.int32, (cap, 1), 0)
    cols = lambda j: pl.ds(pl.multiple_of(j * chunk, chunk), chunk)
    chip_cols = pl.ds(pl.multiple_of(chip * rows, rows), rows)

    def norm(x, branch):
        summed = residual_alpha * x.astype(F32) + branch
        center = summed - jnp.mean(summed, axis=1, keepdims=True)
        inv = lax.rsqrt(jnp.mean(center * center, axis=1, keepdims=True) + NORM_EPS)
        return center * inv, inv

    def forward(k):
        if k == 0:
            loads_a[0].wait()
        else:
            @pl.when(first)
            def _():
                loads_a[k].wait()

            @pl.when(jnp.logical_not(first))
            def _():
                hops_a[k - 1].wait_recv()

        def body(j, _):
            f_hid[:, cols(j)] = gelu(dot(a_in[k], w1[:, cols(j)]), False)[0]
            return 0

        lax.fori_loop(0, chunks, body, 0)
        value = norm(a_in[k], dot_nt(f_hid[...], w2[...]))[0]
        live = row_ids < lengths[me, k - s + sections - 1]
        act_b[k] = jnp.where(live, value, 0.0).astype(BF)
        if k + 1 < ticks:
            @pl.when(jnp.logical_not(last))
            def _():
                hops_a[k].start()
        outs_a[k].start()

    def block(k):
        return pl.ds(k * cap, cap)

    def stage_a(k):
        loads_x[k].wait()
        if k == 0:
            load_w1.wait()

        def body(j, _):
            hidden, slope = gelu(dot(x_in[k], w1[:, cols(j)]), True)
            hid[block(k), cols(j)] = hidden
            slopes[k, :, cols(j)] = slope
            return 0

        lax.fori_loop(0, chunks, body, 0)
        if k == 0:
            load_w2.wait()
        value, inv = norm(x_in[k], dot_nt(hid[block(k), :], w2[...]))
        normed[k] = value
        inv_std[k] = inv
        xt[:, block(k)] = x_in[k, :, chip_cols].T

    def stage_b(k):
        if k == 0:
            loads_c[0].wait()
        else:
            @pl.when(last)
            def _():
                loads_c[k].wait()

            @pl.when(jnp.logical_not(last))
            def _():
                hops_c[k - 1].wait_recv()

        live = row_ids < lengths[me, k + s]
        grad_out = jnp.where(live, c_in[k].astype(F32), 0.0)
        value = normed[k]
        grad_sum = inv_std[k] * (
            grad_out
            - jnp.mean(grad_out, axis=1, keepdims=True)
            - value * jnp.mean(grad_out * value, axis=1, keepdims=True)
        )
        g_b[k] = grad_sum.astype(BF)
        for copy in sends_g[k]:
            copy.start()
        normed[k] = grad_sum

        def body(j, _):
            gp[block(k), cols(j)] = (dot(g_b[k], w2[:, cols(j)]) * slopes[k, :, cols(j)]).astype(BF)
            return 0

        lax.fori_loop(0, chunks, body, 0)
        cot_b[k] = (residual_alpha * normed[k] + dot_nt(gp[block(k), :], w1[...])).astype(BF)
        if k + 1 < ticks:
            @pl.when(jnp.logical_not(first))
            def _():
                hops_c[k].start()
        outs_c[k].start()
        gt[:, block(k)] = g_b[k, :, chip_cols].T

    def stage_r(k):
        for p in range(chips - 1):
            sends_x[k][p].wait_recv()
            sends_g[k][p].wait_recv()
            place = block(ticks + k * (chips - 1) + p)

            def body(j, _):
                hidden, slope = gelu(dot(r_x[k, p], w1[:, cols(j)]), True)
                hid[place, cols(j)] = hidden
                gp[place, cols(j)] = (dot(r_g[k, p], w2[:, cols(j)]) * slope).astype(BF)
                return 0

            lax.fori_loop(0, chunks, body, 0)
            xt[:, place] = r_x[k, p, :, chip_cols].T
            gt[:, place] = r_g[k, p, :, chip_cols].T

    early = (ticks + (ticks - 1) * (chips - 1)) * cap
    terms = ((xt, gp), (gt, hid))

    stage_a(0)
    stage_b(0)
    forward(0)
    for k in range(1, ticks):
        stage_a(k)
    for k in range(1, ticks):
        stage_b(k)
        stage_r(k - 1)
        forward(k)

    for i, (left, right) in enumerate(terms):
        def body(j, _):
            acc[i, :, cols(j)] = dot(left[:, :early], right[:early, cols(j)])
            return 0

        lax.fori_loop(0, chunks, body, 0)

    stage_r(ticks - 1)

    swaps = []
    theirs = pl.ds(pl.multiple_of((1 - core) * own, own), own)
    mine = pl.ds(pl.multiple_of(core * own, own), own)
    for j in range(chunks):
        span = slice(j * chunk, (j + 1) * chunk)
        for i, (left, right) in enumerate(terms):
            if chips > 1:
                acc[i, :, span] += dot(left[:, early:], right[early:, span])
            out_x[j, i] = acc[i, theirs, span].astype(BF)
        swap = pltpu.make_async_remote_copy(
            src_ref=out_x.at[j], dst_ref=in_x.at[j], send_sem=ex_s.at[j], recv_sem=ex_r.at[j],
            device_id={"dp": sibling}, device_id_type=MESH,
        )
        swap.start()
        swaps.append(swap)
    for load in loads_m:
        load.wait()
    stores = []
    for j in range(chunks):
        span = slice(j * chunk, (j + 1) * chunk)
        swaps[j].wait_recv()
        for i, out in enumerate((s1_o, s2_o)):
            grad = acc[i, mine, span] + in_x[j, i].astype(F32)
            moment = beta_one * moments[2 * i, :, span] + (1.0 - beta_one) * grad
            second = beta_two * moments[2 * i + 1, :, span] + (1.0 - beta_two) * grad * grad
            steps[i, :, span] = (moment * (1.0 / correct_one)) / (
                jnp.sqrt(second * (1.0 / correct_two)) + ADAM_EPS
            )
            store = pltpu.make_async_copy(steps.at[i, :, span], out.at[:, span], st_sem.at[j, i])
            store.start()
            stores.append(store)

    for swap in swaps:
        swap.wait_send()
    for copies in sends_x + sends_g:
        for copy in copies:
            copy.wait_send()

    @pl.when(jnp.logical_not(last))
    def _():
        for copy in hops_a:
            copy.wait_send()

    @pl.when(jnp.logical_not(first))
    def _():
        for copy in hops_c:
            copy.wait_send()

    for store in stores + outs_a + outs_c:
        store.wait()


def on_device(*args):
    w_first, lengths, stash = args[0], args[6], args[11]
    sections, groups = lax.axis_size("section"), lax.axis_size("dp")
    ticks, cap, width = stash.shape[2:]
    units = w_first.shape[2]
    chips = groups // 2
    rows, own = width // chips, width // groups
    chunk = 512 if units % 512 == 0 else units
    chunks = units // chunk
    depth = ticks * chips * cap
    dma = pltpu.SemaphoreType.DMA
    vmem = pltpu.VMEM
    remote = (ticks, max(chips - 1, 1))
    anywhere = pl.BlockSpec(memory_space=pl.ANY)
    leave = jax.ShapeDtypeStruct((ticks, cap, width), BF)
    step = jax.ShapeDtypeStruct((own, units), F32)
    act, cot, step_first, step_second = pl.pallas_call(
        functools.partial(kernel, sections, groups, ticks, chunk),
        out_shape=(leave, leave, step, step),
        in_specs=[anywhere] * 6 + [pl.BlockSpec(memory_space=pltpu.SMEM)] + [anywhere] * 5,
        out_specs=(anywhere,) * 4,
        scratch_shapes=[
            vmem((width, units), BF),
            vmem((width, units), BF),
            vmem((4, own, units), F32),
            vmem((ticks, cap, width), BF),
            vmem((ticks, cap, width), BF),
            vmem((ticks, cap, width), BF),
            vmem(remote + (cap, width), BF),
            vmem(remote + (cap, width), BF),
            vmem((ticks, cap, width), BF),
            vmem((ticks, cap, width), BF),
            vmem((ticks, cap, width), BF),
            vmem((ticks, cap, units), F32),
            vmem((ticks, cap, width), F32),
            vmem((ticks, cap, 1), F32),
            vmem((cap, units), BF),
            vmem((depth, units), BF),
            vmem((depth, units), BF),
            vmem((rows, depth), BF),
            vmem((rows, depth), BF),
            vmem((2, rows, units), F32),
            vmem((chunks, 2, own, chunk), BF),
            vmem((chunks, 2, own, chunk), BF),
            vmem((2, own, units), F32),
            dma((2,)),
            dma((4,)),
            dma((ticks,)),
            dma((ticks,)),
            dma((ticks,)),
            dma((2 * ticks,)),
            dma((chunks, 2)),
            dma((2 * ticks,)),
            dma((2 * ticks,)),
            dma(remote),
            dma(remote),
            dma(remote),
            dma(remote),
            dma((chunks,)),
            dma((chunks,)),
        ],
        compiler_params=pltpu.CompilerParams(
            collective_id=0, has_side_effects=True, vmem_limit_bytes=60 * 2**20
        ),
    )(*args)
    return act[None, None], cot[None, None], step_first[None], step_second[None]


def solution(mesh):
    weight, state = P("section", None, None), P("section", "dp", None)
    block, stack = P("dp", "section", None, None), P("dp", "section", None, None, None)
    group = P("dp", None, None, None)
    return jax.shard_map(
        on_device,
        mesh=mesh,
        in_specs=(weight, weight, state, state, state, state, P(), block, block, group, group, stack),
        out_specs=(stack, stack, state, state),
        check_vma=False,
    )
```

```python
import functools

import jax
import jax.numpy as jnp
from jax import lax
from jax.experimental import pallas as pl
from jax.experimental.pallas import tpu as pltpu
from jax.sharding import PartitionSpec as P

NORM_EPS = 1e-05
ADAM_EPS = 1e-08
beta_one = 0.9
beta_two = 0.98
correct_one = 1.0 - 0.9**10
correct_two = 1.0 - 0.98**10
gelu_coeff = 0.7978845608
cubic_coeff = 0.044715
residual_alpha = 1500.0**0.25
NT = (((1,), (1,)), ((), ()))
BF = jnp.bfloat16
F32 = jnp.float32
MESH = pl.DeviceIdType.MESH


def gelu(pre, slope):
    pre = pre.astype(BF)
    square = pre * pre
    tangent = jnp.tanh(pre * (gelu_coeff + (gelu_coeff * cubic_coeff) * square))
    gate = 0.5 * tangent + 0.5
    hidden = pre * gate
    if not slope:
        return hidden, None
    bent = pre * (2.0 * gelu_coeff + (6.0 * gelu_coeff * cubic_coeff) * square)
    return hidden, gate * (1.0 + bent * (1.0 - gate))


def dot(a, b):
    return jnp.dot(a, b, preferred_element_type=F32)


def dot_nt(a, b):
    return lax.dot_general(a, b, NT, preferred_element_type=F32)


def kernel(
    sections, groups, ticks, chunk,
    w1_h, w2_h, m1_h, v1_h, m2_h, v2_h, lengths, act_h, cot_h, embed_h, loss_h, stash_h,
    act_o, cot_o, s1_o, s2_o,
    w1, w2, moments, x_in, a_in, c_in, r_x, r_g, act_b, cot_b, g_b, slopes, normed, inv_std,
    f_hid, hid, gp, xt, gt, acc, out_x, in_x, steps,
    w_sem, mom_sem, x_sem, a_sem, c_sem, o_sem, st_sem,
    hop_s, hop_r, rx_s, rx_r, rg_s, rg_r, ex_s, ex_r,
):
    s = lax.axis_index("section")
    me = lax.axis_index("dp")
    chips = groups // 2
    chip, core = me // 2, me % 2
    sibling = me + 1 - 2 * core
    width, units = w1.shape
    cap = x_in.shape[1]
    rows = width // chips
    own = rows // 2
    chunks = units // chunk
    first, last = s == 0, s == sections - 1
    nxt = jnp.minimum(s + 1, sections - 1)
    prv = jnp.maximum(s - 1, 0)
    partners = [lax.rem(chip + p, chips) * 2 + core for p in range(1, chips)]

    barrier = pltpu.get_barrier_semaphore()

    @pl.when(jnp.logical_not(first))
    def _():
        pl.semaphore_signal(barrier, inc=1, device_id={"section": prv}, device_id_type=MESH)

    @pl.when(jnp.logical_not(last))
    def _():
        pl.semaphore_signal(barrier, inc=1, device_id={"section": nxt}, device_id_type=MESH)

    for other in partners + [sibling]:
        pl.semaphore_signal(barrier, inc=1, device_id={"dp": other}, device_id_type=MESH)

    loads_x = [pltpu.make_async_copy(stash_h.at[0, 0, k], x_in.at[k], x_sem.at[k]) for k in range(ticks)]
    load_w1 = pltpu.make_async_copy(w1_h.at[0], w1, w_sem.at[0])
    load_w2 = pltpu.make_async_copy(w2_h.at[0], w2, w_sem.at[1])
    loads_a = [pltpu.make_async_copy(act_h.at[0, 0], a_in.at[0], a_sem.at[0])]
    loads_c = [pltpu.make_async_copy(cot_h.at[0, 0], c_in.at[0], c_sem.at[0])]
    for k in range(1, ticks):
        loads_a.append(pltpu.make_async_copy(embed_h.at[0, k - 1], a_in.at[k], a_sem.at[k]))
        loads_c.append(pltpu.make_async_copy(loss_h.at[0, k - 1], c_in.at[k], c_sem.at[k]))
    loads_m = [
        pltpu.make_async_copy(h.at[0], moments.at[i], mom_sem.at[i])
        for i, h in enumerate((m1_h, v1_h, m2_h, v2_h))
    ]
    loads_x[0].start()
    load_w1.start()
    load_w2.start()
    loads_c[0].start()
    loads_a[0].start()
    for k in range(1, ticks):
        loads_x[k].start()

    @pl.when(first)
    def _():
        for k in range(1, ticks):
            loads_a[k].start()

    @pl.when(last)
    def _():
        for k in range(1, ticks):
            loads_c[k].start()

    for load in loads_m:
        load.start()

    pl.semaphore_wait(
        barrier, chips + jnp.where(first, 0, 1) + jnp.where(last, 0, 1)
    )

    def send_tick(k, src, dst, send, recv):
        return [
            pltpu.make_async_remote_copy(
                src_ref=src, dst_ref=dst.at[k, p], send_sem=send.at[k, p], recv_sem=recv.at[k, p],
                device_id={"dp": other}, device_id_type=MESH,
            )
            for p, other in enumerate(partners)
        ]

    sends_x = [send_tick(k, stash_h.at[0, 0, k], r_x, rx_s, rx_r) for k in range(ticks)]
    sends_g = [send_tick(k, g_b.at[k], r_g, rg_s, rg_r) for k in range(ticks)]
    for copies in sends_x:
        for copy in copies:
            copy.start()

    def hop(src, dst, i, to):
        return pltpu.make_async_remote_copy(
            src_ref=src, dst_ref=dst, send_sem=hop_s.at[i], recv_sem=hop_r.at[i],
            device_id={"section": to}, device_id_type=MESH,
        )

    hops_a = [hop(act_b.at[k], a_in.at[k + 1], k, nxt) for k in range(ticks - 1)]
    hops_c = [hop(cot_b.at[k], c_in.at[k + 1], ticks - 1 + k, prv) for k in range(ticks - 1)]
    outs_a = [pltpu.make_async_copy(act_b.at[k], act_o.at[k], o_sem.at[k]) for k in range(ticks)]
    outs_c = [pltpu.make_async_copy(cot_b.at[k], cot_o.at[k], o_sem.at[ticks + k]) for k in range(ticks)]

    row_ids = lax.broadcasted_iota(jnp.int32, (cap, 1), 0)
    cols = lambda j: pl.ds(pl.multiple_of(j * chunk, chunk), chunk)
    chip_cols = pl.ds(pl.multiple_of(chip * rows, rows), rows)

    def norm(x, branch):
        summed = residual_alpha * x.astype(F32) + branch
        center = summed - jnp.mean(summed, axis=1, keepdims=True)
        inv = lax.rsqrt(jnp.mean(center * center, axis=1, keepdims=True) + NORM_EPS)
        return center * inv, inv

    def forward(k):
        if k == 0:
            loads_a[0].wait()
        else:
            @pl.when(first)
            def _():
                loads_a[k].wait()

            @pl.when(jnp.logical_not(first))
            def _():
                hops_a[k - 1].wait_recv()

        def body(j, _):
            f_hid[:, cols(j)] = gelu(dot(a_in[k], w1[:, cols(j)]), False)[0]
            return 0

        lax.fori_loop(0, chunks, body, 0, unroll=2)
        value = norm(a_in[k], dot_nt(f_hid[...], w2[...]))[0]
        live = row_ids < lengths[me, k - s + sections - 1]
        act_b[k] = jnp.where(live, value, 0.0).astype(BF)
        if k + 1 < ticks:
            @pl.when(jnp.logical_not(last))
            def _():
                hops_a[k].start()
        outs_a[k].start()

    def block(k):
        return pl.ds(k * cap, cap)

    def stage_a(k):
        loads_x[k].wait()
        if k == 0:
            load_w1.wait()

        def body(j, _):
            hidden, slope = gelu(dot(x_in[k], w1[:, cols(j)]), True)
            hid[block(k), cols(j)] = hidden
            slopes[k, :, cols(j)] = slope
            return 0

        lax.fori_loop(0, chunks, body, 0, unroll=2)
        if k == 0:
            load_w2.wait()
        value, inv = norm(x_in[k], dot_nt(hid[block(k), :], w2[...]))
        normed[k] = value
        inv_std[k] = inv
        xt[:, block(k)] = x_in[k, :, chip_cols].T

    def stage_b(k):
        if k == 0:
            loads_c[0].wait()
        else:
            @pl.when(last)
            def _():
                loads_c[k].wait()

            @pl.when(jnp.logical_not(last))
            def _():
                hops_c[k - 1].wait_recv()

        live = row_ids < lengths[me, k + s]
        grad_out = jnp.where(live, c_in[k].astype(F32), 0.0)
        value = normed[k]
        grad_sum = inv_std[k] * (
            grad_out
            - jnp.mean(grad_out, axis=1, keepdims=True)
            - value * jnp.mean(grad_out * value, axis=1, keepdims=True)
        )
        g_b[k] = grad_sum.astype(BF)
        for copy in sends_g[k]:
            copy.start()
        normed[k] = grad_sum

        def body(j, _):
            gp[block(k), cols(j)] = dot(g_b[k], w2[:, cols(j)]).astype(BF) * slopes[k, :, cols(j)]
            return 0

        lax.fori_loop(0, chunks, body, 0, unroll=2)
        cot_b[k] = (residual_alpha * normed[k] + dot_nt(gp[block(k), :], w1[...])).astype(BF)
        if k + 1 < ticks:
            @pl.when(jnp.logical_not(first))
            def _():
                hops_c[k].start()
        outs_c[k].start()
        gt[:, block(k)] = g_b[k, :, chip_cols].T

    def stage_r(k):
        for p in range(chips - 1):
            sends_x[k][p].wait_recv()
            sends_g[k][p].wait_recv()
            place = block(ticks + k * (chips - 1) + p)

            def body(j, _):
                hidden, slope = gelu(dot(r_x[k, p], w1[:, cols(j)]), True)
                hid[place, cols(j)] = hidden
                gp[place, cols(j)] = dot(r_g[k, p], w2[:, cols(j)]).astype(BF) * slope
                return 0

            lax.fori_loop(0, chunks, body, 0, unroll=2)
            xt[:, place] = r_x[k, p, :, chip_cols].T
            gt[:, place] = r_g[k, p, :, chip_cols].T

    early = (ticks + (ticks - 1) * (chips - 1)) * cap
    terms = ((xt, gp), (gt, hid))

    stage_a(0)
    stage_b(0)
    forward(0)
    for k in range(1, ticks):
        stage_a(k)
    for k in range(1, ticks):
        stage_b(k)
        stage_r(k - 1)
        forward(k)

    for i, (left, right) in enumerate(terms):
        def body(j, _):
            acc[i, :, cols(j)] = dot(left[:, :early], right[:early, cols(j)])
            return 0

        lax.fori_loop(0, chunks, body, 0, unroll=2)

    stage_r(ticks - 1)

    swaps = []
    theirs = pl.ds(pl.multiple_of((1 - core) * own, own), own)
    mine = pl.ds(pl.multiple_of(core * own, own), own)
    for j in range(chunks):
        span = slice(j * chunk, (j + 1) * chunk)
        for i, (left, right) in enumerate(terms):
            if chips > 1:
                acc[i, :, span] += dot(left[:, early:], right[early:, span])
            out_x[j, i] = acc[i, theirs, span].astype(BF)
        swap = pltpu.make_async_remote_copy(
            src_ref=out_x.at[j], dst_ref=in_x.at[j], send_sem=ex_s.at[j], recv_sem=ex_r.at[j],
            device_id={"dp": sibling}, device_id_type=MESH,
        )
        swap.start()
        swaps.append(swap)
    for load in loads_m:
        load.wait()
    stores = []
    for j in range(chunks):
        span = slice(j * chunk, (j + 1) * chunk)
        swaps[j].wait_recv()
        for i, out in enumerate((s1_o, s2_o)):
            grad = acc[i, mine, span] + in_x[j, i].astype(F32)
            moment = beta_one * moments[2 * i, :, span] + (1.0 - beta_one) * grad
            second = beta_two * moments[2 * i + 1, :, span] + (1.0 - beta_two) * grad * grad
            steps[i, :, span] = (moment * (1.0 / correct_one)) / (
                jnp.sqrt(second * (1.0 / correct_two)) + ADAM_EPS
            )
            store = pltpu.make_async_copy(steps.at[i, :, span], out.at[:, span], st_sem.at[j, i])
            store.start()
            stores.append(store)

    for swap in swaps:
        swap.wait_send()
    for copies in sends_x + sends_g:
        for copy in copies:
            copy.wait_send()

    @pl.when(jnp.logical_not(last))
    def _():
        for copy in hops_a:
            copy.wait_send()

    @pl.when(jnp.logical_not(first))
    def _():
        for copy in hops_c:
            copy.wait_send()

    for store in stores + outs_a + outs_c:
        store.wait()


def hand_over(*refs):
    count = len(refs) // 2
    sem = refs[-1]
    copies, used = [], 0
    for src, dst in zip(refs[:count], refs[count : 2 * count]):
        if len(src.shape) == 3:
            spans = list(range(src.shape[0]))
        else:
            part = src.shape[0] // 4
            spans = [pl.ds(i * part, part) for i in range(4)]
        for span in spans:
            copies.append(pltpu.make_async_copy(src.at[span], dst.at[span], sem.at[used]))
            used += 1
    for copy in copies:
        copy.start()
    for copy in copies:
        copy.wait()


def on_device(*args):
    w_first, lengths, stash = args[0], args[6], args[11]
    sections, groups = lax.axis_size("section"), lax.axis_size("dp")
    ticks, cap, width = stash.shape[2:]
    units = w_first.shape[2]
    chips = groups // 2
    rows, own = width // chips, width // groups
    chunk = 512 if units % 512 == 0 else units
    chunks = units // chunk
    depth = ticks * chips * cap
    dma = pltpu.SemaphoreType.DMA
    vmem = pltpu.VMEM
    remote = (ticks, max(chips - 1, 1))
    anywhere = pl.BlockSpec(memory_space=pl.ANY)
    leave = jax.ShapeDtypeStruct((ticks, cap, width), BF)
    step = jax.ShapeDtypeStruct((own, units), F32)
    made = pl.pallas_call(
        functools.partial(kernel, sections, groups, ticks, chunk),
        out_shape=(leave, leave, step, step),
        in_specs=[anywhere] * 6 + [pl.BlockSpec(memory_space=pltpu.SMEM)] + [anywhere] * 5,
        out_specs=(anywhere,) * 4,
        scratch_shapes=[
            vmem((width, units), BF),
            vmem((width, units), BF),
            vmem((4, own, units), F32),
            vmem((ticks, cap, width), BF),
            vmem((ticks, cap, width), BF),
            vmem((ticks, cap, width), BF),
            vmem(remote + (cap, width), BF),
            vmem(remote + (cap, width), BF),
            vmem((ticks, cap, width), BF),
            vmem((ticks, cap, width), BF),
            vmem((ticks, cap, width), BF),
            vmem((ticks, cap, units), BF),
            vmem((ticks, cap, width), F32),
            vmem((ticks, cap, 1), F32),
            vmem((cap, units), BF),
            vmem((depth, units), BF),
            vmem((depth, units), BF),
            vmem((rows, depth), BF),
            vmem((rows, depth), BF),
            vmem((2, rows, units), F32),
            vmem((chunks, 2, own, chunk), BF),
            vmem((chunks, 2, own, chunk), BF),
            vmem((2, own, units), F32),
            dma((2,)),
            dma((4,)),
            dma((ticks,)),
            dma((ticks,)),
            dma((ticks,)),
            dma((2 * ticks,)),
            dma((chunks, 2)),
            dma((2 * ticks,)),
            dma((2 * ticks,)),
            dma(remote),
            dma(remote),
            dma(remote),
            dma(remote),
            dma((chunks,)),
            dma((chunks,)),
        ],
        compiler_params=pltpu.CompilerParams(
            collective_id=0, has_side_effects=True, vmem_limit_bytes=60 * 2**20
        ),
    )(*args)
    act, cot, step_first, step_second = pl.pallas_call(
        hand_over,
        out_shape=(leave, leave, step, step),
        in_specs=[anywhere] * 4,
        out_specs=(anywhere,) * 4,
        scratch_shapes=[dma((2 * ticks + 8,))],
        compiler_params=pltpu.CompilerParams(vmem_limit_bytes=60 * 2**20),
    )(*made)
    return act[None, None], cot[None, None], step_first[None], step_second[None]


def solution(mesh):
    weight, state = P("section", None, None), P("section", "dp", None)
    block, stack = P("dp", "section", None, None), P("dp", "section", None, None, None)
    group = P("dp", None, None, None)
    return jax.shard_map(
        on_device,
        mesh=mesh,
        in_specs=(weight, weight, state, state, state, state, P(), block, block, group, group, stack),
        out_specs=(stack, stack, state, state),
        check_vma=False,
    )
```

```python
import functools

import jax
import jax.numpy as jnp
from jax import lax
from jax.experimental import pallas as pl
from jax.experimental.pallas import tpu as pltpu
from jax.sharding import PartitionSpec as P

NORM_EPS = 1e-05
ADAM_EPS = 1e-08
beta_one = 0.9
beta_two = 0.98
correct_one = 1.0 - 0.9**10
correct_two = 1.0 - 0.98**10
gelu_coeff = 0.7978845608
cubic_coeff = 0.044715
residual_alpha = 1500.0**0.25
NT = (((1,), (1,)), ((), ()))
BF = jnp.bfloat16
F32 = jnp.float32
MESH = pl.DeviceIdType.MESH


def gelu(pre, slope):
    pre = pre.astype(BF)
    square = pre * pre
    tangent = jnp.tanh(pre * (gelu_coeff + (gelu_coeff * cubic_coeff) * square))
    gate = 0.5 * tangent + 0.5
    hidden = pre * gate
    if not slope:
        return hidden, None
    bent = pre * (2.0 * gelu_coeff + (6.0 * gelu_coeff * cubic_coeff) * square)
    return hidden, gate * (1.0 + bent * (1.0 - gate))


def dot(a, b):
    return jnp.dot(a, b, preferred_element_type=F32)


def dot_nt(a, b):
    return lax.dot_general(a, b, NT, preferred_element_type=F32)


def kernel(
    sections, groups, ticks, chunk,
    w1_h, w2_h, m1_h, v1_h, m2_h, v2_h, lengths, act_h, cot_h, embed_h, loss_h, stash_h,
    act_o, cot_o, s1_o, s2_o,
    w1, w2, moments, x_in, a_in, c_in, r_x, r_g, act_b, cot_b, g_b, slopes, r_slope, normed, inv_std,
    f_hid, hid, gp, xt, gt, acc, out_x, in_x, steps,
    w_sem, mom_sem, x_sem, a_sem, c_sem, o_sem, st_sem,
    hop_s, hop_r, rx_s, rx_r, rg_s, rg_r, ex_s, ex_r,
):
    s = lax.axis_index("section")
    me = lax.axis_index("dp")
    chips = groups // 2
    chip, core = me // 2, me % 2
    sibling = me + 1 - 2 * core
    width, units = w1.shape
    cap = x_in.shape[1]
    rows = width // chips
    own = rows // 2
    chunks = units // chunk
    first, last = s == 0, s == sections - 1
    nxt = jnp.minimum(s + 1, sections - 1)
    prv = jnp.maximum(s - 1, 0)
    partners = [lax.rem(chip + p, chips) * 2 + core for p in range(1, chips)]

    barrier = pltpu.get_barrier_semaphore()

    @pl.when(jnp.logical_not(first))
    def _():
        pl.semaphore_signal(barrier, inc=1, device_id={"section": prv}, device_id_type=MESH)

    @pl.when(jnp.logical_not(last))
    def _():
        pl.semaphore_signal(barrier, inc=1, device_id={"section": nxt}, device_id_type=MESH)

    for other in partners + [sibling]:
        pl.semaphore_signal(barrier, inc=1, device_id={"dp": other}, device_id_type=MESH)

    loads_x = [pltpu.make_async_copy(stash_h.at[0, 0, k], x_in.at[k], x_sem.at[k]) for k in range(ticks)]
    load_w1 = pltpu.make_async_copy(w1_h.at[0], w1, w_sem.at[0])
    load_w2 = pltpu.make_async_copy(w2_h.at[0], w2, w_sem.at[1])
    loads_a = [pltpu.make_async_copy(act_h.at[0, 0], a_in.at[0], a_sem.at[0])]
    loads_c = [pltpu.make_async_copy(cot_h.at[0, 0], c_in.at[0], c_sem.at[0])]
    for k in range(1, ticks):
        loads_a.append(pltpu.make_async_copy(embed_h.at[0, k - 1], a_in.at[k], a_sem.at[k]))
        loads_c.append(pltpu.make_async_copy(loss_h.at[0, k - 1], c_in.at[k], c_sem.at[k]))
    loads_m = [
        pltpu.make_async_copy(h.at[0], moments.at[i], mom_sem.at[i])
        for i, h in enumerate((m1_h, v1_h, m2_h, v2_h))
    ]
    loads_x[0].start()
    load_w1.start()
    load_w2.start()
    loads_c[0].start()
    loads_a[0].start()
    for k in range(1, ticks):
        loads_x[k].start()

    @pl.when(first)
    def _():
        for k in range(1, ticks):
            loads_a[k].start()

    @pl.when(last)
    def _():
        for k in range(1, ticks):
            loads_c[k].start()

    for load in loads_m:
        load.start()

    pl.semaphore_wait(
        barrier, chips + jnp.where(first, 0, 1) + jnp.where(last, 0, 1)
    )

    def send_tick(k, src, dst, send, recv):
        return [
            pltpu.make_async_remote_copy(
                src_ref=src, dst_ref=dst.at[k, p], send_sem=send.at[k, p], recv_sem=recv.at[k, p],
                device_id={"dp": other}, device_id_type=MESH,
            )
            for p, other in enumerate(partners)
        ]

    sends_x = [send_tick(k, stash_h.at[0, 0, k], r_x, rx_s, rx_r) for k in range(ticks)]
    sends_g = [send_tick(k, g_b.at[k], r_g, rg_s, rg_r) for k in range(ticks)]
    for copy in sends_x[0]:
        copy.start()

    def hop(src, dst, i, to):
        return pltpu.make_async_remote_copy(
            src_ref=src, dst_ref=dst, send_sem=hop_s.at[i], recv_sem=hop_r.at[i],
            device_id={"section": to}, device_id_type=MESH,
        )

    hops_a = [hop(act_b.at[k], a_in.at[k + 1], k, nxt) for k in range(ticks - 1)]
    hops_c = [hop(cot_b.at[k], c_in.at[k + 1], ticks - 1 + k, prv) for k in range(ticks - 1)]
    outs_a = [pltpu.make_async_copy(act_b.at[k], act_o.at[k], o_sem.at[k]) for k in range(ticks)]
    outs_c = [pltpu.make_async_copy(cot_b.at[k], cot_o.at[k], o_sem.at[ticks + k]) for k in range(ticks)]

    row_ids = lax.broadcasted_iota(jnp.int32, (cap, 1), 0)
    cols = lambda j: pl.ds(pl.multiple_of(j * chunk, chunk), chunk)
    chip_cols = pl.ds(pl.multiple_of(chip * rows, rows), rows)

    def norm(x, branch):
        summed = residual_alpha * x.astype(F32) + branch
        center = summed - jnp.mean(summed, axis=1, keepdims=True)
        inv = lax.rsqrt(jnp.mean(center * center, axis=1, keepdims=True) + NORM_EPS)
        return center * inv, inv

    def forward(k):
        if k == 0:
            loads_a[0].wait()
        else:
            @pl.when(first)
            def _():
                loads_a[k].wait()

            @pl.when(jnp.logical_not(first))
            def _():
                hops_a[k - 1].wait_recv()

        def body(j, _):
            f_hid[:, cols(j)] = gelu(dot(a_in[k], w1[:, cols(j)]), False)[0]
            return 0

        lax.fori_loop(0, chunks, body, 0, unroll=2)
        value = norm(a_in[k], dot_nt(f_hid[...], w2[...]))[0]
        live = row_ids < lengths[me, k - s + sections - 1]
        act_b[k] = jnp.where(live, value, 0.0).astype(BF)
        if k + 1 < ticks:
            @pl.when(jnp.logical_not(last))
            def _():
                hops_a[k].start()
        outs_a[k].start()

    def block(k):
        return pl.ds(k * cap, cap)

    def stage_a(k):
        loads_x[k].wait()
        if k == 0:
            load_w1.wait()

        def body(j, _):
            hidden, slope = gelu(dot(x_in[k], w1[:, cols(j)]), True)
            hid[block(k), cols(j)] = hidden
            slopes[k, :, cols(j)] = slope
            return 0

        lax.fori_loop(0, chunks, body, 0, unroll=2)
        if k == 0:
            load_w2.wait()
        value, inv = norm(x_in[k], dot_nt(hid[block(k), :], w2[...]))
        normed[k] = value
        inv_std[k] = inv
        xt[:, block(k)] = x_in[k, :, chip_cols].T

    def stage_b(k):
        if k == 0:
            loads_c[0].wait()
        else:
            @pl.when(last)
            def _():
                loads_c[k].wait()

            @pl.when(jnp.logical_not(last))
            def _():
                hops_c[k - 1].wait_recv()

        live = row_ids < lengths[me, k + s]
        grad_out = jnp.where(live, c_in[k].astype(F32), 0.0)
        value = normed[k]
        grad_sum = inv_std[k] * (
            grad_out
            - jnp.mean(grad_out, axis=1, keepdims=True)
            - value * jnp.mean(grad_out * value, axis=1, keepdims=True)
        )
        g_b[k] = grad_sum.astype(BF)
        for copy in sends_g[k] + (sends_x[k + 1] if k + 1 < ticks else []):
            copy.start()
        normed[k] = grad_sum

        def body(j, _):
            gp[block(k), cols(j)] = dot(g_b[k], w2[:, cols(j)]).astype(BF) * slopes[k, :, cols(j)]
            return 0

        lax.fori_loop(0, chunks, body, 0, unroll=2)
        cot_b[k] = (residual_alpha * normed[k] + dot_nt(gp[block(k), :], w1[...])).astype(BF)
        if k + 1 < ticks:
            @pl.when(jnp.logical_not(first))
            def _():
                hops_c[k].start()
        outs_c[k].start()
        gt[:, block(k)] = g_b[k, :, chip_cols].T

    def place(k, p):
        return block(ticks + k * (chips - 1) + p)

    def stage_rx(k):
        for p in range(chips - 1):
            sends_x[k][p].wait_recv()

            def body(j, _):
                hidden, slope = gelu(dot(r_x[k, p], w1[:, cols(j)]), True)
                hid[place(k, p), cols(j)] = hidden
                r_slope[p, :, cols(j)] = slope
                return 0

            lax.fori_loop(0, chunks, body, 0, unroll=2)
            xt[:, place(k, p)] = r_x[k, p, :, chip_cols].T

    def stage_rg(k):
        for p in range(chips - 1):
            sends_g[k][p].wait_recv()
            gt[:, place(k, p)] = r_g[k, p, :, chip_cols].T

    def remote_gp(k, p, span):
        gp[place(k, p), span] = dot(r_g[k, p], w2[:, span]).astype(BF) * r_slope[p, :, span]

    early = (ticks + (ticks - 1) * (chips - 1)) * cap
    terms = ((xt, gp), (gt, hid))

    stage_a(0)
    stage_b(0)
    forward(0)
    for k in range(1, ticks):
        stage_a(k)
    for k in range(1, ticks):
        stage_rx(k - 1)
        stage_b(k)
        stage_rg(k - 1)
        for p in range(chips - 1):
            def body(j, _):
                remote_gp(k - 1, p, cols(j))
                return 0

            lax.fori_loop(0, chunks, body, 0, unroll=2)
        forward(k)
    stage_rx(ticks - 1)

    for i, (left, right) in enumerate(terms):
        def body(j, _):
            acc[i, :, cols(j)] = dot(left[:, :early], right[:early, cols(j)])
            return 0

        lax.fori_loop(0, chunks, body, 0, unroll=2)

    stage_rg(ticks - 1)

    swaps = []
    theirs = pl.ds(pl.multiple_of((1 - core) * own, own), own)
    mine = pl.ds(pl.multiple_of(core * own, own), own)
    for j in range(chunks):
        span = slice(j * chunk, (j + 1) * chunk)
        for p in range(chips - 1):
            remote_gp(ticks - 1, p, span)
        for i, (left, right) in enumerate(terms):
            if chips > 1:
                acc[i, :, span] += dot(left[:, early:], right[early:, span])
            out_x[j, i] = acc[i, theirs, span].astype(BF)
        swap = pltpu.make_async_remote_copy(
            src_ref=out_x.at[j], dst_ref=in_x.at[j], send_sem=ex_s.at[j], recv_sem=ex_r.at[j],
            device_id={"dp": sibling}, device_id_type=MESH,
        )
        swap.start()
        swaps.append(swap)
    for load in loads_m:
        load.wait()
    stores = []
    for j in range(chunks):
        span = slice(j * chunk, (j + 1) * chunk)
        swaps[j].wait_recv()
        for i, out in enumerate((s1_o, s2_o)):
            grad = acc[i, mine, span] + in_x[j, i].astype(F32)
            moment = beta_one * moments[2 * i, :, span] + (1.0 - beta_one) * grad
            second = beta_two * moments[2 * i + 1, :, span] + (1.0 - beta_two) * grad * grad
            steps[i, :, span] = (moment * (1.0 / correct_one)) / (
                jnp.sqrt(second * (1.0 / correct_two)) + ADAM_EPS
            )
            store = pltpu.make_async_copy(steps.at[i, :, span], out.at[:, span], st_sem.at[j, i])
            store.start()
            stores.append(store)

    for swap in swaps:
        swap.wait_send()
    for copies in sends_x + sends_g:
        for copy in copies:
            copy.wait_send()

    @pl.when(jnp.logical_not(last))
    def _():
        for copy in hops_a:
            copy.wait_send()

    @pl.when(jnp.logical_not(first))
    def _():
        for copy in hops_c:
            copy.wait_send()

    for store in stores + outs_a + outs_c:
        store.wait()


def hand_over(*refs):
    sources, results, held, sems = refs[:4], refs[4:8], refs[8:12], refs[12]
    loads, stores = [], []
    for src, dst, buf in zip(sources, results, held):
        if len(src.shape) == 3:
            spans = list(range(src.shape[0]))
        else:
            part = src.shape[0] // 4
            spans = [pl.ds(i * part, part) for i in range(4)]
        for span in spans:
            loads.append(pltpu.make_async_copy(src.at[span], buf.at[span], sems.at[0, len(loads)]))
            stores.append(pltpu.make_async_copy(buf.at[span], dst.at[span], sems.at[1, len(stores)]))
    for load in loads:
        load.start()
    for load, store in zip(loads, stores):
        load.wait()
        store.start()
    for store in stores:
        store.wait()


def on_device(*args):
    w_first, lengths, stash = args[0], args[6], args[11]
    sections, groups = lax.axis_size("section"), lax.axis_size("dp")
    ticks, cap, width = stash.shape[2:]
    units = w_first.shape[2]
    chips = groups // 2
    rows, own = width // chips, width // groups
    chunk = 512 if units % 512 == 0 else units
    chunks = units // chunk
    depth = ticks * chips * cap
    dma = pltpu.SemaphoreType.DMA
    vmem = pltpu.VMEM
    remote = (ticks, max(chips - 1, 1))
    anywhere = pl.BlockSpec(memory_space=pl.ANY)
    leave = jax.ShapeDtypeStruct((ticks, cap, width), BF)
    step = jax.ShapeDtypeStruct((own, units), F32)
    made = pl.pallas_call(
        functools.partial(kernel, sections, groups, ticks, chunk),
        out_shape=(leave, leave, step, step),
        in_specs=[anywhere] * 6 + [pl.BlockSpec(memory_space=pltpu.SMEM)] + [anywhere] * 5,
        out_specs=(anywhere,) * 4,
        scratch_shapes=[
            vmem((width, units), BF),
            vmem((width, units), BF),
            vmem((4, own, units), F32),
            vmem((ticks, cap, width), BF),
            vmem((ticks, cap, width), BF),
            vmem((ticks, cap, width), BF),
            vmem(remote + (cap, width), BF),
            vmem(remote + (cap, width), BF),
            vmem((ticks, cap, width), BF),
            vmem((ticks, cap, width), BF),
            vmem((ticks, cap, width), BF),
            vmem((ticks, cap, units), BF),
            vmem((max(chips - 1, 1), cap, units), BF),
            vmem((ticks, cap, width), F32),
            vmem((ticks, cap, 1), F32),
            vmem((cap, units), BF),
            vmem((depth, units), BF),
            vmem((depth, units), BF),
            vmem((rows, depth), BF),
            vmem((rows, depth), BF),
            vmem((2, rows, units), F32),
            vmem((chunks, 2, own, chunk), BF),
            vmem((chunks, 2, own, chunk), BF),
            vmem((2, own, units), F32),
            dma((2,)),
            dma((4,)),
            dma((ticks,)),
            dma((ticks,)),
            dma((ticks,)),
            dma((2 * ticks,)),
            dma((chunks, 2)),
            dma((2 * ticks,)),
            dma((2 * ticks,)),
            dma(remote),
            dma(remote),
            dma(remote),
            dma(remote),
            dma((chunks,)),
            dma((chunks,)),
        ],
        compiler_params=pltpu.CompilerParams(
            collective_id=0, has_side_effects=True, vmem_limit_bytes=60 * 2**20
        ),
    )(*args)
    act, cot, step_first, step_second = pl.pallas_call(
        hand_over,
        out_shape=(leave, leave, step, step),
        in_specs=[anywhere] * 4,
        out_specs=(anywhere,) * 4,
        scratch_shapes=[
            vmem(leave.shape, BF),
            vmem(leave.shape, BF),
            vmem(step.shape, F32),
            vmem(step.shape, F32),
            dma((2, 2 * ticks + 8)),
        ],
        compiler_params=pltpu.CompilerParams(vmem_limit_bytes=60 * 2**20),
    )(*made)
    return act[None, None], cot[None, None], step_first[None], step_second[None]


def solution(mesh):
    weight, state = P("section", None, None), P("section", "dp", None)
    block, stack = P("dp", "section", None, None), P("dp", "section", None, None, None)
    group = P("dp", None, None, None)
    return jax.shard_map(
        on_device,
        mesh=mesh,
        in_specs=(weight, weight, state, state, state, state, P(), block, block, group, group, stack),
        out_specs=(stack, stack, state, state),
        check_vma=False,
    )
```

```python
import functools

import jax
import jax.numpy as jnp
from jax import lax
from jax.experimental import pallas as pl
from jax.experimental.pallas import tpu as pltpu
from jax.sharding import PartitionSpec as P

NORM_EPS = 1e-05
ADAM_EPS = 1e-08
beta_one = 0.9
beta_two = 0.98
correct_one = 1.0 - 0.9**10
correct_two = 1.0 - 0.98**10
gelu_coeff = 0.7978845608
cubic_coeff = 0.044715
residual_alpha = 1500.0**0.25
NT = (((1,), (1,)), ((), ()))
BF = jnp.bfloat16
F32 = jnp.float32
MESH = pl.DeviceIdType.MESH


def gelu(pre, slope):
    pre = pre.astype(BF)
    square = pre * pre
    tangent = jnp.tanh(pre * (gelu_coeff + (gelu_coeff * cubic_coeff) * square))
    gate = 0.5 * tangent + 0.5
    hidden = pre * gate
    if not slope:
        return hidden, None
    bent = pre * (2.0 * gelu_coeff + (6.0 * gelu_coeff * cubic_coeff) * square)
    return hidden, gate * (1.0 + bent * (1.0 - gate))


def dot(a, b):
    return jnp.dot(a, b, preferred_element_type=F32)


def dot_nt(a, b):
    return lax.dot_general(a, b, NT, preferred_element_type=F32)


def kernel(
    sections, groups, ticks, chunk,
    w1_h, w2_h, m1_h, v1_h, m2_h, v2_h, lengths, act_h, cot_h, embed_h, loss_h, stash_h,
    act_o, cot_o, s1_o, s2_o,
    w1, w2, moments, x_in, a_in, c_in, r_x, r_g, act_b, cot_b, g_b, slopes, r_slope, normed, inv_std,
    f_hid, hid, gp, xt, gt, acc, out_x, in_x, steps,
    w_sem, mom_sem, x_sem, a_sem, c_sem, o_sem, st_sem,
    hop_s, hop_r, rx_s, rx_r, rg_s, rg_r, ex_s, ex_r,
):
    s = lax.axis_index("section")
    me = lax.axis_index("dp")
    chips = groups // 2
    chip, core = me // 2, me % 2
    sibling = me + 1 - 2 * core
    width, units = w1.shape
    cap = x_in.shape[1]
    rows = width // chips
    own = rows // 2
    chunks = units // chunk
    first, last = s == 0, s == sections - 1
    nxt = jnp.minimum(s + 1, sections - 1)
    prv = jnp.maximum(s - 1, 0)
    partners = [lax.rem(chip + p, chips) * 2 + core for p in range(1, chips)]

    barrier = pltpu.get_barrier_semaphore()

    @pl.when(jnp.logical_not(first))
    def _():
        pl.semaphore_signal(barrier, inc=1, device_id={"section": prv}, device_id_type=MESH)

    @pl.when(jnp.logical_not(last))
    def _():
        pl.semaphore_signal(barrier, inc=1, device_id={"section": nxt}, device_id_type=MESH)

    for other in partners + [sibling]:
        pl.semaphore_signal(barrier, inc=1, device_id={"dp": other}, device_id_type=MESH)

    loads_x = [pltpu.make_async_copy(stash_h.at[0, 0, k], x_in.at[k], x_sem.at[k]) for k in range(ticks)]
    load_w1 = pltpu.make_async_copy(w1_h.at[0], w1, w_sem.at[0])
    load_w2 = pltpu.make_async_copy(w2_h.at[0], w2, w_sem.at[1])
    loads_a = [pltpu.make_async_copy(act_h.at[0, 0], a_in.at[0], a_sem.at[0])]
    loads_c = [pltpu.make_async_copy(cot_h.at[0, 0], c_in.at[0], c_sem.at[0])]
    for k in range(1, ticks):
        loads_a.append(pltpu.make_async_copy(embed_h.at[0, k - 1], a_in.at[k], a_sem.at[k]))
        loads_c.append(pltpu.make_async_copy(loss_h.at[0, k - 1], c_in.at[k], c_sem.at[k]))
    loads_m = [
        pltpu.make_async_copy(h.at[0], moments.at[i], mom_sem.at[i])
        for i, h in enumerate((m1_h, v1_h, m2_h, v2_h))
    ]
    loads_x[0].start()
    load_w1.start()
    load_w2.start()
    loads_c[0].start()
    loads_a[0].start()
    for k in range(1, ticks):
        loads_x[k].start()

    @pl.when(first)
    def _():
        for k in range(1, ticks):
            loads_a[k].start()

    @pl.when(last)
    def _():
        for k in range(1, ticks):
            loads_c[k].start()

    for load in loads_m:
        load.start()

    pl.semaphore_wait(
        barrier, chips + jnp.where(first, 0, 1) + jnp.where(last, 0, 1)
    )

    def send_tick(k, src, dst, send, recv):
        return [
            pltpu.make_async_remote_copy(
                src_ref=src, dst_ref=dst.at[k, p], send_sem=send.at[k, p], recv_sem=recv.at[k, p],
                device_id={"dp": other}, device_id_type=MESH,
            )
            for p, other in enumerate(partners)
        ]

    sends_x = [send_tick(k, stash_h.at[0, 0, k], r_x, rx_s, rx_r) for k in range(ticks)]
    sends_g = [send_tick(k, g_b.at[k], r_g, rg_s, rg_r) for k in range(ticks)]
    for copy in sends_x[0]:
        copy.start()

    def hop(src, dst, i, to):
        return pltpu.make_async_remote_copy(
            src_ref=src, dst_ref=dst, send_sem=hop_s.at[i], recv_sem=hop_r.at[i],
            device_id={"section": to}, device_id_type=MESH,
        )

    hops_a = [hop(act_b.at[k], a_in.at[k + 1], k, nxt) for k in range(ticks - 1)]
    hops_c = [hop(cot_b.at[k], c_in.at[k + 1], ticks - 1 + k, prv) for k in range(ticks - 1)]
    outs_a = [pltpu.make_async_copy(act_b.at[k], act_o.at[k], o_sem.at[k]) for k in range(ticks)]
    outs_c = [pltpu.make_async_copy(cot_b.at[k], cot_o.at[k], o_sem.at[ticks + k]) for k in range(ticks)]

    row_ids = lax.broadcasted_iota(jnp.int32, (cap, 1), 0)
    cols = lambda j: pl.ds(pl.multiple_of(j * chunk, chunk), chunk)
    chip_cols = pl.ds(pl.multiple_of(chip * rows, rows), rows)

    def norm(x, branch):
        summed = residual_alpha * x.astype(F32) + branch
        center = summed - jnp.mean(summed, axis=1, keepdims=True)
        inv = lax.rsqrt(jnp.mean(center * center, axis=1, keepdims=True) + NORM_EPS)
        return center * inv, inv

    def forward(k):
        if k == 0:
            loads_a[0].wait()
        else:
            @pl.when(first)
            def _():
                loads_a[k].wait()

            @pl.when(jnp.logical_not(first))
            def _():
                hops_a[k - 1].wait_recv()

        def body(j, _):
            f_hid[:, cols(j)] = gelu(dot(a_in[k], w1[:, cols(j)]), False)[0]
            return 0

        lax.fori_loop(0, chunks, body, 0, unroll=2)
        value = norm(a_in[k], dot_nt(f_hid[...], w2[...]))[0]
        live = row_ids < lengths[me, k - s + sections - 1]
        act_b[k] = jnp.where(live, value, 0.0).astype(BF)
        if k + 1 < ticks:
            @pl.when(jnp.logical_not(last))
            def _():
                hops_a[k].start()
        outs_a[k].start()

    def block(k):
        return pl.ds(k * cap, cap)

    def stage_a(k):
        loads_x[k].wait()
        if k == 0:
            load_w1.wait()

        def body(j, _):
            hidden, slope = gelu(dot(x_in[k], w1[:, cols(j)]), True)
            hid[block(k), cols(j)] = hidden
            slopes[k, :, cols(j)] = slope
            return 0

        lax.fori_loop(0, chunks, body, 0, unroll=2)
        if k == 0:
            load_w2.wait()
        value, inv = norm(x_in[k], dot_nt(hid[block(k), :], w2[...]))
        normed[k] = value
        inv_std[k] = inv
        xt[:, block(k)] = x_in[k, :, chip_cols].T

    def stage_b(k):
        if k == 0:
            loads_c[0].wait()
        else:
            @pl.when(last)
            def _():
                loads_c[k].wait()

            @pl.when(jnp.logical_not(last))
            def _():
                hops_c[k - 1].wait_recv()

        live = row_ids < lengths[me, k + s]
        grad_out = jnp.where(live, c_in[k].astype(F32), 0.0)
        value = normed[k]
        grad_sum = inv_std[k] * (
            grad_out
            - jnp.mean(grad_out, axis=1, keepdims=True)
            - value * jnp.mean(grad_out * value, axis=1, keepdims=True)
        )
        g_b[k] = grad_sum.astype(BF)
        for copy in sends_g[k] + (sends_x[k + 1] if k + 1 < ticks else []):
            copy.start()
        normed[k] = grad_sum

        def body(j, _):
            gp[block(k), cols(j)] = dot(g_b[k], w2[:, cols(j)]).astype(BF) * slopes[k, :, cols(j)]
            return 0

        lax.fori_loop(0, chunks, body, 0, unroll=2)
        cot_b[k] = (residual_alpha * normed[k] + dot_nt(gp[block(k), :], w1[...])).astype(BF)
        if k + 1 < ticks:
            @pl.when(jnp.logical_not(first))
            def _():
                hops_c[k].start()
        outs_c[k].start()
        gt[:, block(k)] = g_b[k, :, chip_cols].T

    def place(k, p):
        return block(ticks + k * (chips - 1) + p)

    def stage_rx(k):
        for p in range(chips - 1):
            sends_x[k][p].wait_recv()

            def body(j, _):
                hidden, slope = gelu(dot(r_x[k, p], w1[:, cols(j)]), True)
                hid[place(k, p), cols(j)] = hidden
                r_slope[p, :, cols(j)] = slope
                return 0

            lax.fori_loop(0, chunks, body, 0, unroll=2)
            xt[:, place(k, p)] = r_x[k, p, :, chip_cols].T

    def stage_rg(k):
        for p in range(chips - 1):
            sends_g[k][p].wait_recv()
            gt[:, place(k, p)] = r_g[k, p, :, chip_cols].T

    def remote_gp(k, p, span):
        gp[place(k, p), span] = dot(r_g[k, p], w2[:, span]).astype(BF) * r_slope[p, :, span]

    early = (ticks + (ticks - 1) * (chips - 1)) * cap
    terms = ((xt, gp), (gt, hid))

    def remote_products(k):
        for p in range(chips - 1):
            def body(j, _):
                remote_gp(k, p, cols(j))
                return 0

            lax.fori_loop(0, chunks, body, 0, unroll=2)

    stage_a(0)
    stage_b(0)
    for k in range(1, ticks):
        stage_a(k)
    forward(0)
    stage_b(1)
    stage_rx(0)
    for k in range(2, ticks):
        stage_rg(k - 2)
        remote_products(k - 2)
        stage_rx(k - 1)
        forward(k - 1)
        stage_b(k)
    stage_rg(ticks - 2)
    remote_products(ticks - 2)

    for i, (left, right) in enumerate(terms):
        def body(j, _):
            acc[i, :, cols(j)] = dot(left[:, :early], right[:early, cols(j)])
            return 0

        lax.fori_loop(0, chunks, body, 0, unroll=2)

    stage_rx(ticks - 1)
    forward(ticks - 1)
    stage_rg(ticks - 1)

    swaps = []
    theirs = pl.ds(pl.multiple_of((1 - core) * own, own), own)
    mine = pl.ds(pl.multiple_of(core * own, own), own)
    for j in range(chunks):
        span = slice(j * chunk, (j + 1) * chunk)
        for p in range(chips - 1):
            remote_gp(ticks - 1, p, span)
        for i, (left, right) in enumerate(terms):
            if chips > 1:
                acc[i, :, span] += dot(left[:, early:], right[early:, span])
            out_x[j, i] = acc[i, theirs, span].astype(BF)
        swap = pltpu.make_async_remote_copy(
            src_ref=out_x.at[j], dst_ref=in_x.at[j], send_sem=ex_s.at[j], recv_sem=ex_r.at[j],
            device_id={"dp": sibling}, device_id_type=MESH,
        )
        swap.start()
        swaps.append(swap)
    for load in loads_m:
        load.wait()
    stores = []
    for j in range(chunks):
        span = slice(j * chunk, (j + 1) * chunk)
        swaps[j].wait_recv()
        for i, out in enumerate((s1_o, s2_o)):
            grad = acc[i, mine, span] + in_x[j, i].astype(F32)
            moment = beta_one * moments[2 * i, :, span] + (1.0 - beta_one) * grad
            second = beta_two * moments[2 * i + 1, :, span] + (1.0 - beta_two) * grad * grad
            steps[i, :, span] = (moment * (1.0 / correct_one)) / (
                jnp.sqrt(second * (1.0 / correct_two)) + ADAM_EPS
            )
            store = pltpu.make_async_copy(steps.at[i, :, span], out.at[:, span], st_sem.at[j, i])
            store.start()
            stores.append(store)

    for swap in swaps:
        swap.wait_send()
    for copies in sends_x + sends_g:
        for copy in copies:
            copy.wait_send()

    @pl.when(jnp.logical_not(last))
    def _():
        for copy in hops_a:
            copy.wait_send()

    @pl.when(jnp.logical_not(first))
    def _():
        for copy in hops_c:
            copy.wait_send()

    for store in stores + outs_a + outs_c:
        store.wait()


def hand_over(*refs):
    sources, results, held, sems = refs[:4], refs[4:8], refs[8:12], refs[12]
    loads, stores = [], []
    for src, dst, buf in zip(sources, results, held):
        if len(src.shape) == 3:
            spans = list(range(src.shape[0]))
        else:
            part = src.shape[0] // 4
            spans = [pl.ds(i * part, part) for i in range(4)]
        for span in spans:
            loads.append(pltpu.make_async_copy(src.at[span], buf.at[span], sems.at[0, len(loads)]))
            stores.append(pltpu.make_async_copy(buf.at[span], dst.at[span], sems.at[1, len(stores)]))
    for load in loads:
        load.start()
    for load, store in zip(loads, stores):
        load.wait()
        store.start()
    for store in stores:
        store.wait()


def on_device(*args):
    w_first, lengths, stash = args[0], args[6], args[11]
    sections, groups = lax.axis_size("section"), lax.axis_size("dp")
    ticks, cap, width = stash.shape[2:]
    units = w_first.shape[2]
    chips = groups // 2
    rows, own = width // chips, width // groups
    chunk = 512 if units % 512 == 0 else units
    chunks = units // chunk
    depth = ticks * chips * cap
    dma = pltpu.SemaphoreType.DMA
    vmem = pltpu.VMEM
    remote = (ticks, max(chips - 1, 1))
    anywhere = pl.BlockSpec(memory_space=pl.ANY)
    leave = jax.ShapeDtypeStruct((ticks, cap, width), BF)
    step = jax.ShapeDtypeStruct((own, units), F32)
    made = pl.pallas_call(
        functools.partial(kernel, sections, groups, ticks, chunk),
        out_shape=(leave, leave, step, step),
        in_specs=[anywhere] * 6 + [pl.BlockSpec(memory_space=pltpu.SMEM)] + [anywhere] * 5,
        out_specs=(anywhere,) * 4,
        scratch_shapes=[
            vmem((width, units), BF),
            vmem((width, units), BF),
            vmem((4, own, units), F32),
            vmem((ticks, cap, width), BF),
            vmem((ticks, cap, width), BF),
            vmem((ticks, cap, width), BF),
            vmem(remote + (cap, width), BF),
            vmem(remote + (cap, width), BF),
            vmem((ticks, cap, width), BF),
            vmem((ticks, cap, width), BF),
            vmem((ticks, cap, width), BF),
            vmem((ticks, cap, units), BF),
            vmem((max(chips - 1, 1), cap, units), BF),
            vmem((ticks, cap, width), F32),
            vmem((ticks, cap, 1), F32),
            vmem((cap, units), BF),
            vmem((depth, units), BF),
            vmem((depth, units), BF),
            vmem((rows, depth), BF),
            vmem((rows, depth), BF),
            vmem((2, rows, units), F32),
            vmem((chunks, 2, own, chunk), BF),
            vmem((chunks, 2, own, chunk), BF),
            vmem((2, own, units), F32),
            dma((2,)),
            dma((4,)),
            dma((ticks,)),
            dma((ticks,)),
            dma((ticks,)),
            dma((2 * ticks,)),
            dma((chunks, 2)),
            dma((2 * ticks,)),
            dma((2 * ticks,)),
            dma(remote),
            dma(remote),
            dma(remote),
            dma(remote),
            dma((chunks,)),
            dma((chunks,)),
        ],
        compiler_params=pltpu.CompilerParams(
            collective_id=0, has_side_effects=True, vmem_limit_bytes=60 * 2**20
        ),
    )(*args)
    act, cot, step_first, step_second = pl.pallas_call(
        hand_over,
        out_shape=(leave, leave, step, step),
        in_specs=[anywhere] * 4,
        out_specs=(anywhere,) * 4,
        scratch_shapes=[
            vmem(leave.shape, BF),
            vmem(leave.shape, BF),
            vmem(step.shape, F32),
            vmem(step.shape, F32),
            dma((2, 2 * ticks + 8)),
        ],
        compiler_params=pltpu.CompilerParams(vmem_limit_bytes=60 * 2**20),
    )(*made)
    return act[None, None], cot[None, None], step_first[None], step_second[None]


def solution(mesh):
    weight, state = P("section", None, None), P("section", "dp", None)
    block, stack = P("dp", "section", None, None), P("dp", "section", None, None, None)
    group = P("dp", None, None, None)
    return jax.shard_map(
        on_device,
        mesh=mesh,
        in_specs=(weight, weight, state, state, state, state, P(), block, block, group, group, stack),
        out_specs=(stack, stack, state, state),
        check_vma=False,
    )
```

```python
import functools

import jax
import jax.numpy as jnp
from jax import lax
from jax.experimental import pallas as pl
from jax.experimental.pallas import tpu as pltpu
from jax.sharding import PartitionSpec as P

NORM_EPS = 1e-05
ADAM_EPS = 1e-08
beta_one = 0.9
beta_two = 0.98
correct_one = 1.0 - 0.9**10
correct_two = 1.0 - 0.98**10
gelu_coeff = 0.7978845608
cubic_coeff = 0.044715
residual_alpha = 1500.0**0.25
NT = (((1,), (1,)), ((), ()))
BF = jnp.bfloat16
F32 = jnp.float32
MESH = pl.DeviceIdType.MESH


def gelu(pre, slope):
    pre = pre.astype(BF)
    square = pre * pre
    tangent = jnp.tanh(pre * (gelu_coeff + (gelu_coeff * cubic_coeff) * square))
    gate = 0.5 * tangent + 0.5
    hidden = pre * gate
    if not slope:
        return hidden, None
    bent = pre * (2.0 * gelu_coeff + (6.0 * gelu_coeff * cubic_coeff) * square)
    return hidden, gate * (1.0 + bent * (1.0 - gate))


def dot(a, b):
    return jnp.dot(a, b, preferred_element_type=F32)


def dot_nt(a, b):
    return lax.dot_general(a, b, NT, preferred_element_type=F32)


def kernel(
    sections, groups, ticks, chunk,
    w1_h, w2_h, m1_h, v1_h, m2_h, v2_h, lengths, act_h, cot_h, embed_h, loss_h, stash_h,
    act_o, cot_o, s1_o, s2_o,
    w1, w2, moments, x_in, a_in, c_in, r_x, r_g, act_b, cot_b, g_b, slopes, r_slope, normed, inv_std,
    f_hid, hid, gp, xt, gt, acc, out_x, in_x, steps,
    w_sem, mom_sem, x_sem, a_sem, c_sem, o_sem, st_sem,
    hop_s, hop_r, rx_s, rx_r, rg_s, rg_r, ex_s, ex_r,
):
    s = lax.axis_index("section")
    me = lax.axis_index("dp")
    chips = groups // 2
    chip, core = me // 2, me % 2
    sibling = me + 1 - 2 * core
    width, units = w1.shape
    cap = x_in.shape[1]
    rows = width // chips
    own = rows // 2
    chunks = units // chunk
    first, last = s == 0, s == sections - 1
    nxt = jnp.minimum(s + 1, sections - 1)
    prv = jnp.maximum(s - 1, 0)
    partners = [lax.rem(chip + p, chips) * 2 + core for p in range(1, chips)]

    barrier = pltpu.get_barrier_semaphore()

    @pl.when(jnp.logical_not(first))
    def _():
        pl.semaphore_signal(barrier, inc=1, device_id={"section": prv}, device_id_type=MESH)

    @pl.when(jnp.logical_not(last))
    def _():
        pl.semaphore_signal(barrier, inc=1, device_id={"section": nxt}, device_id_type=MESH)

    for other in partners + [sibling]:
        pl.semaphore_signal(barrier, inc=1, device_id={"dp": other}, device_id_type=MESH)

    loads_x = [pltpu.make_async_copy(stash_h.at[0, 0, k], x_in.at[k], x_sem.at[k]) for k in range(ticks)]
    load_w1 = pltpu.make_async_copy(w1_h.at[0], w1, w_sem.at[0])
    load_w2 = pltpu.make_async_copy(w2_h.at[0], w2, w_sem.at[1])
    loads_a = [pltpu.make_async_copy(act_h.at[0, 0], a_in.at[0], a_sem.at[0])]
    loads_c = [pltpu.make_async_copy(cot_h.at[0, 0], c_in.at[0], c_sem.at[0])]
    for k in range(1, ticks):
        loads_a.append(pltpu.make_async_copy(embed_h.at[0, k - 1], a_in.at[k], a_sem.at[k]))
        loads_c.append(pltpu.make_async_copy(loss_h.at[0, k - 1], c_in.at[k], c_sem.at[k]))
    loads_m = [
        pltpu.make_async_copy(h.at[0], moments.at[i], mom_sem.at[i])
        for i, h in enumerate((m1_h, v1_h, m2_h, v2_h))
    ]
    loads_x[0].start()
    load_w1.start()
    load_w2.start()
    loads_c[0].start()
    loads_a[0].start()
    for k in range(1, ticks):
        loads_x[k].start()

    @pl.when(first)
    def _():
        for k in range(1, ticks):
            loads_a[k].start()

    @pl.when(last)
    def _():
        for k in range(1, ticks):
            loads_c[k].start()

    for load in loads_m:
        load.start()

    pl.semaphore_wait(
        barrier, chips + jnp.where(first, 0, 1) + jnp.where(last, 0, 1)
    )

    def send_tick(k, src, dst, send, recv):
        return [
            pltpu.make_async_remote_copy(
                src_ref=src, dst_ref=dst.at[k, p], send_sem=send.at[k, p], recv_sem=recv.at[k, p],
                device_id={"dp": other}, device_id_type=MESH,
            )
            for p, other in enumerate(partners)
        ]

    sends_x = [send_tick(k, stash_h.at[0, 0, k], r_x, rx_s, rx_r) for k in range(ticks)]
    sends_g = [send_tick(k, g_b.at[k], r_g, rg_s, rg_r) for k in range(ticks)]
    for copy in sends_x[0]:
        copy.start()

    def hop(src, dst, i, to):
        return pltpu.make_async_remote_copy(
            src_ref=src, dst_ref=dst, send_sem=hop_s.at[i], recv_sem=hop_r.at[i],
            device_id={"section": to}, device_id_type=MESH,
        )

    hops_a = [hop(act_b.at[k], a_in.at[k + 1], k, nxt) for k in range(ticks - 1)]
    hops_c = [hop(cot_b.at[k], c_in.at[k + 1], ticks - 1 + k, prv) for k in range(ticks - 1)]
    outs_a = [pltpu.make_async_copy(act_b.at[k], act_o.at[k], o_sem.at[k]) for k in range(ticks)]
    outs_c = [pltpu.make_async_copy(cot_b.at[k], cot_o.at[k], o_sem.at[ticks + k]) for k in range(ticks)]

    row_ids = lax.broadcasted_iota(jnp.int32, (cap, 1), 0)
    cols = lambda j: pl.ds(pl.multiple_of(j * chunk, chunk), chunk)
    chip_cols = pl.ds(pl.multiple_of(chip * rows, rows), rows)

    def norm(x, branch):
        summed = residual_alpha * x.astype(F32) + branch
        center = summed - jnp.mean(summed, axis=1, keepdims=True)
        inv = lax.rsqrt(jnp.mean(center * center, axis=1, keepdims=True) + NORM_EPS)
        return center * inv, inv

    def forward(k):
        if k == 0:
            loads_a[0].wait()
        else:
            @pl.when(first)
            def _():
                loads_a[k].wait()

            @pl.when(jnp.logical_not(first))
            def _():
                hops_a[k - 1].wait_recv()

        def body(j, _):
            f_hid[:, cols(j)] = gelu(dot(a_in[k], w1[:, cols(j)]), False)[0]
            return 0

        lax.fori_loop(0, chunks, body, 0, unroll=2)
        value = norm(a_in[k], dot_nt(f_hid[...], w2[...]))[0]
        live = row_ids < lengths[me, k - s + sections - 1]
        act_b[k] = jnp.where(live, value, 0.0).astype(BF)
        if k + 1 < ticks:
            @pl.when(jnp.logical_not(last))
            def _():
                hops_a[k].start()
        outs_a[k].start()

    def block(k):
        return pl.ds(k * cap, cap)

    def stage_a(k):
        loads_x[k].wait()
        if k == 0:
            load_w1.wait()

        def body(j, _):
            hidden, slope = gelu(dot(x_in[k], w1[:, cols(j)]), True)
            hid[block(k), cols(j)] = hidden
            slopes[k, :, cols(j)] = slope
            return 0

        lax.fori_loop(0, chunks, body, 0, unroll=2)
        if k == 0:
            load_w2.wait()
        value, inv = norm(x_in[k], dot_nt(hid[block(k), :], w2[...]))
        normed[k] = value
        inv_std[k] = inv
        xt[:, block(k)] = x_in[k, :, chip_cols].T

    def stage_b(k):
        if k == 0:
            loads_c[0].wait()
        else:
            @pl.when(last)
            def _():
                loads_c[k].wait()

            @pl.when(jnp.logical_not(last))
            def _():
                hops_c[k - 1].wait_recv()

        live = row_ids < lengths[me, k + s]
        grad_out = jnp.where(live, c_in[k].astype(F32), 0.0)
        value = normed[k]
        grad_sum = inv_std[k] * (
            grad_out
            - jnp.mean(grad_out, axis=1, keepdims=True)
            - value * jnp.mean(grad_out * value, axis=1, keepdims=True)
        )
        g_b[k] = grad_sum.astype(BF)
        for copy in sends_g[k] + (sum(sends_x[1:], []) if k == 0 else []):
            copy.start()
        normed[k] = grad_sum

        def body(j, _):
            gp[block(k), cols(j)] = dot(g_b[k], w2[:, cols(j)]).astype(BF) * slopes[k, :, cols(j)]
            return 0

        lax.fori_loop(0, chunks, body, 0, unroll=2)
        cot_b[k] = (residual_alpha * normed[k] + dot_nt(gp[block(k), :], w1[...])).astype(BF)
        if k + 1 < ticks:
            @pl.when(jnp.logical_not(first))
            def _():
                hops_c[k].start()
        outs_c[k].start()
        gt[:, block(k)] = g_b[k, :, chip_cols].T

    def place(k, p):
        return block(ticks + k * (chips - 1) + p)

    def stage_rx(k):
        for p in range(chips - 1):
            sends_x[k][p].wait_recv()

            def body(j, _):
                hidden, slope = gelu(dot(r_x[k, p], w1[:, cols(j)]), True)
                hid[place(k, p), cols(j)] = hidden
                r_slope[p, :, cols(j)] = slope
                return 0

            lax.fori_loop(0, chunks, body, 0, unroll=2)
            xt[:, place(k, p)] = r_x[k, p, :, chip_cols].T

    def stage_rg(k):
        for p in range(chips - 1):
            sends_g[k][p].wait_recv()
            gt[:, place(k, p)] = r_g[k, p, :, chip_cols].T

    def remote_gp(k, p, span):
        gp[place(k, p), span] = dot(r_g[k, p], w2[:, span]).astype(BF) * r_slope[p, :, span]

    early = (ticks + (ticks - 1) * (chips - 1)) * cap
    terms = ((xt, gp), (gt, hid))

    def remote_products(k):
        for p in range(chips - 1):
            def body(j, _):
                remote_gp(k, p, cols(j))
                return 0

            lax.fori_loop(0, chunks, body, 0, unroll=2)

    stage_a(0)
    stage_b(0)
    for k in range(1, ticks):
        stage_a(k)
    forward(0)
    stage_b(1)
    stage_rx(0)
    for k in range(2, ticks):
        stage_rg(k - 2)
        remote_products(k - 2)
        stage_rx(k - 1)
        forward(k - 1)
        stage_b(k)
    stage_rg(ticks - 2)
    remote_products(ticks - 2)

    for i, (left, right) in enumerate(terms):
        def body(j, _):
            acc[i, :, cols(j)] = dot(left[:, :early], right[:early, cols(j)])
            return 0

        lax.fori_loop(0, chunks, body, 0, unroll=2)

    stage_rx(ticks - 1)
    forward(ticks - 1)
    stage_rg(ticks - 1)

    swaps = []
    theirs = pl.ds(pl.multiple_of((1 - core) * own, own), own)
    mine = pl.ds(pl.multiple_of(core * own, own), own)
    for j in range(chunks):
        span = slice(j * chunk, (j + 1) * chunk)
        for p in range(chips - 1):
            remote_gp(ticks - 1, p, span)
        for i, (left, right) in enumerate(terms):
            if chips > 1:
                acc[i, :, span] += dot(left[:, early:], right[early:, span])
            out_x[j, i] = acc[i, theirs, span].astype(BF)
        swap = pltpu.make_async_remote_copy(
            src_ref=out_x.at[j], dst_ref=in_x.at[j], send_sem=ex_s.at[j], recv_sem=ex_r.at[j],
            device_id={"dp": sibling}, device_id_type=MESH,
        )
        swap.start()
        swaps.append(swap)
    for load in loads_m:
        load.wait()
    stores = []
    for j in range(chunks):
        span = slice(j * chunk, (j + 1) * chunk)
        swaps[j].wait_recv()
        for i, out in enumerate((s1_o, s2_o)):
            grad = acc[i, mine, span] + in_x[j, i].astype(F32)
            moment = beta_one * moments[2 * i, :, span] + (1.0 - beta_one) * grad
            second = beta_two * moments[2 * i + 1, :, span] + (1.0 - beta_two) * grad * grad
            steps[i, :, span] = (moment * (1.0 / correct_one)) / (
                jnp.sqrt(second * (1.0 / correct_two)) + ADAM_EPS
            )
            store = pltpu.make_async_copy(steps.at[i, :, span], out.at[:, span], st_sem.at[j, i])
            store.start()
            stores.append(store)

    for swap in swaps:
        swap.wait_send()
    for copies in sends_x + sends_g:
        for copy in copies:
            copy.wait_send()

    @pl.when(jnp.logical_not(last))
    def _():
        for copy in hops_a:
            copy.wait_send()

    @pl.when(jnp.logical_not(first))
    def _():
        for copy in hops_c:
            copy.wait_send()

    for store in stores + outs_a + outs_c:
        store.wait()


def hand_over(*refs):
    sources, results, held, sems = refs[:4], refs[4:8], refs[8:12], refs[12]
    loads, stores = [], []
    for src, dst, buf in zip(sources, results, held):
        if len(src.shape) == 3:
            spans = list(range(src.shape[0]))
        else:
            part = src.shape[0] // 4
            spans = [pl.ds(i * part, part) for i in range(4)]
        for span in spans:
            loads.append(pltpu.make_async_copy(src.at[span], buf.at[span], sems.at[0, len(loads)]))
            stores.append(pltpu.make_async_copy(buf.at[span], dst.at[span], sems.at[1, len(stores)]))
    for load in loads:
        load.start()
    for load, store in zip(loads, stores):
        load.wait()
        store.start()
    for store in stores:
        store.wait()


def on_device(*args):
    w_first, lengths, stash = args[0], args[6], args[11]
    sections, groups = lax.axis_size("section"), lax.axis_size("dp")
    ticks, cap, width = stash.shape[2:]
    units = w_first.shape[2]
    chips = groups // 2
    rows, own = width // chips, width // groups
    chunk = 512 if units % 512 == 0 else units
    chunks = units // chunk
    depth = ticks * chips * cap
    dma = pltpu.SemaphoreType.DMA
    vmem = pltpu.VMEM
    remote = (ticks, max(chips - 1, 1))
    anywhere = pl.BlockSpec(memory_space=pl.ANY)
    leave = jax.ShapeDtypeStruct((ticks, cap, width), BF)
    step = jax.ShapeDtypeStruct((own, units), F32)
    made = pl.pallas_call(
        functools.partial(kernel, sections, groups, ticks, chunk),
        out_shape=(leave, leave, step, step),
        in_specs=[anywhere] * 6 + [pl.BlockSpec(memory_space=pltpu.SMEM)] + [anywhere] * 5,
        out_specs=(anywhere,) * 4,
        scratch_shapes=[
            vmem((width, units), BF),
            vmem((width, units), BF),
            vmem((4, own, units), F32),
            vmem((ticks, cap, width), BF),
            vmem((ticks, cap, width), BF),
            vmem((ticks, cap, width), BF),
            vmem(remote + (cap, width), BF),
            vmem(remote + (cap, width), BF),
            vmem((ticks, cap, width), BF),
            vmem((ticks, cap, width), BF),
            vmem((ticks, cap, width), BF),
            vmem((ticks, cap, units), BF),
            vmem((max(chips - 1, 1), cap, units), BF),
            vmem((ticks, cap, width), F32),
            vmem((ticks, cap, 1), F32),
            vmem((cap, units), BF),
            vmem((depth, units), BF),
            vmem((depth, units), BF),
            vmem((rows, depth), BF),
            vmem((rows, depth), BF),
            vmem((2, rows, units), F32),
            vmem((chunks, 2, own, chunk), BF),
            vmem((chunks, 2, own, chunk), BF),
            vmem((2, own, units), F32),
            dma((2,)),
            dma((4,)),
            dma((ticks,)),
            dma((ticks,)),
            dma((ticks,)),
            dma((2 * ticks,)),
            dma((chunks, 2)),
            dma((2 * ticks,)),
            dma((2 * ticks,)),
            dma(remote),
            dma(remote),
            dma(remote),
            dma(remote),
            dma((chunks,)),
            dma((chunks,)),
        ],
        compiler_params=pltpu.CompilerParams(
            collective_id=0, has_side_effects=True, vmem_limit_bytes=60 * 2**20
        ),
    )(*args)
    act, cot, step_first, step_second = pl.pallas_call(
        hand_over,
        out_shape=(leave, leave, step, step),
        in_specs=[anywhere] * 4,
        out_specs=(anywhere,) * 4,
        scratch_shapes=[
            vmem(leave.shape, BF),
            vmem(leave.shape, BF),
            vmem(step.shape, F32),
            vmem(step.shape, F32),
            dma((2, 2 * ticks + 8)),
        ],
        compiler_params=pltpu.CompilerParams(vmem_limit_bytes=60 * 2**20),
    )(*made)
    return act[None, None], cot[None, None], step_first[None], step_second[None]


def solution(mesh):
    weight, state = P("section", None, None), P("section", "dp", None)
    block, stack = P("dp", "section", None, None), P("dp", "section", None, None, None)
    group = P("dp", None, None, None)
    return jax.shard_map(
        on_device,
        mesh=mesh,
        in_specs=(weight, weight, state, state, state, state, P(), block, block, group, group, stack),
        out_specs=(stack, stack, state, state),
        check_vma=False,
    )
```
